32 devices in a mesh: groups: 2 (over y), segment: 4 (over z), dp: 4 (over x, core).
Axes of the slice: x: 2, y: 2, z: 4, core: 2. Of those that a mesh axis runs over, the one named last changes fastest.
Arguments:
- layer_input: bfloat16 [16, 4, 32, 2560], P('groups', 'dp'), parts along dimension 0, may hold values from -6 to 6
- attn_gain: float32 [4, 2560], P('segment'), may hold values from 0.5 to 1.5
- qkv_weight: bfloat16 [4, 2560, 3584], P('segment', 'dp')
- final_gain: float32 [2560], replicated, may hold values from 0.5 to 1.5
- head_weight: bfloat16 [2560, 10240], P('dp', 'segment')
- vocab_blocks: int32 [16, 2, 4], P('groups'), parts along dimension 0, may hold values from 0 to 79, as said below
- languages: int32 [16, 4, 32], P('groups', 'dp'), parts along dimension 0, may hold values from 0 to 1
- targets: int32 [16, 4, 32], P('groups', 'dp'), parts along dimension 0, may hold values from 0 to 511
- teacher: bfloat16 [16, 4, 32, 512], P('groups', 'dp'), parts along dimension 0, may hold values from 1.9431114e-05 to 0.0078125
Outputs:
- kl_loss: float32 [16, 4, 32], P('groups', 'dp'), parts along dimension 0
- ce_loss: float32 [16, 4, 32], P('groups', 'dp'), parts along dimension 0
The draws below stay inside these ranges and needn't reach their ends.
There are 2 independent parts, one for each index of `groups`. The reference program is written for one: setup_inputs(seed, part) draws one part's arguments, and reference() takes and returns one part's arrays. A program takes and returns all parts, laid end to end along the dimension named above; an argument that names none is the same for every part. Nothing has to cross between parts.
Inputs may be any that keep to these rules, and one draw needn't show every extreme that they name: `vocab_blocks`: each list names 4 different blocks. Section s holds blocks s * 20 to (s + 1) * 20 - 1; at most 2 blocks of one list lie in one section, and for every list some section holds exactly 2.
All inputs are finite; a program needn't handle non-finite values.
Results may differ from the reference program's by a relative error of at most 0.01.
Values may be sent and summed in bfloat16 or wider, within the bound.
No kernel may reach another device: no remote copies, remote signals or barrier semaphores. Data moves between devices by JAX's collectives and lax.ppermute only.
A program may use at most 128 MiB of HBM per device.

```python
import math
import jax
import jax.numpy as jnp
from jax import lax

D = 2560
HEAD = 128
QHEADS = 20
KVHEADS = 4
BLOCK = 128
VB_SEGMENT = 20
CAP = 2
LANGS = 2
MB = 8
SEQ = 32
SEL = 4
N_SEGMENT = 4
N_DP = 4


def draw_qkv_weight(key, part):
    key = jax.random.fold_in(key, 11)
    noise_key = jax.random.fold_in(key, 0)
    full_width = QHEADS * HEAD + 2 * KVHEADS * HEAD
    base_draw = jax.random.normal(noise_key, (N_SEGMENT, D, full_width), jnp.float32) * D ** (-0.5)
    return base_draw.astype(jnp.bfloat16)


def draw_head_weight(key, part):
    key = jax.random.fold_in(key, 13)
    noise_key = jax.random.fold_in(key, 0)
    width_all = VB_SEGMENT * BLOCK * N_SEGMENT
    base_draw = jax.random.normal(noise_key, (D, width_all), jnp.float32) * D ** (-0.5)
    return base_draw.astype(jnp.bfloat16)


def draw_vocab_blocks(key, part):
    key = jax.random.fold_in(key, 17)
    home_key, base_key, perm_key = jax.random.split(key, 3)
    list_count = MB * LANGS
    home_section = jax.random.randint(home_key, (list_count, 1), 0, N_SEGMENT)
    offsets = jax.random.randint(base_key, (list_count, N_SEGMENT), 0, VB_SEGMENT)
    places = jnp.arange(SEL, dtype=jnp.int32)[None, :]
    rest = places - CAP
    in_home = places < CAP
    others = N_SEGMENT - 1
    section_ids = jnp.where(in_home, home_section, (home_section + 1 + jnp.maximum(rest, 0) % others) % N_SEGMENT)
    step_ids = jnp.where(in_home, places, jnp.maximum(rest, 0) // others)
    local_ids = (jnp.take_along_axis(offsets, section_ids, axis=1) + step_ids) % VB_SEGMENT
    block_ids = section_ids * VB_SEGMENT + local_ids
    orders = jax.vmap(lambda sub_key: jax.random.permutation(sub_key, SEL))(jax.random.split(perm_key, list_count))
    block_ids = jnp.take_along_axis(block_ids, orders.astype(jnp.int32), axis=1)
    return block_ids.reshape(MB, LANGS, SEL).astype(jnp.int32)


def plant(result, stream_key, low, top_value):
    index_at = [jax.random.randint(jax.random.fold_in(stream_key, axis), (), 0, length) for axis, length in enumerate(result.shape)]
    longest = result.shape.index(max(result.shape))
    next_to = index_at[:longest] + [(index_at[longest] + 1) % result.shape[longest]] + index_at[longest + 1:]
    return result.at[tuple(index_at)].set(low).at[tuple(next_to)].set(top_value)


def levels(rng, extent, shards, smallest, largest):
    def one(axis_at, blocks):
        steps = jax.random.uniform(jax.random.fold_in(jax.random.fold_in(rng, 6), axis_at), (blocks,), jnp.float32, smallest / len(shards), largest / len(shards))
        return jnp.repeat(jnp.exp(steps), extent[axis_at] // blocks).reshape((-1,) + (1,) * (len(extent) - axis_at - 1))

    factor_of = one(*shards[0])
    for cut in shards[1:]:
        factor_of = factor_of * one(*cut)
    return factor_of


def normal_values(rng, shape, deviation, most, cuts=(), held_as=jnp.bfloat16):
    array = jax.random.normal(rng, shape, jnp.float32) * deviation
    if len(cuts) > 0:
        array = levels(rng, shape, cuts, -0.22, 0.18) * array
    return jnp.clip(array, min=-most, max=most).astype(held_as)


def setup_inputs(seed: int = 0, part: int = 0) -> dict:
    splits = jax.random.split(jax.random.key(seed), 10)
    part_splits = jax.random.split(jax.random.fold_in(splits[9], part), 10)
    layer_input = normal_values(part_splits[0], (MB, N_DP, SEQ, D), 1.0, 6.0, ((1, 4),))
    attn_gain = jnp.clip(1.0 + 0.1 * jax.random.normal(splits[1], (N_SEGMENT, D), jnp.float32), 0.5, 1.5)
    qkv_weight = draw_qkv_weight(jax.random.fold_in(splits[9], 71), part)
    final_gain = jnp.clip(1.0 + 0.1 * jax.random.normal(splits[3], (D,), jnp.float32), 0.5, 1.5)
    head_weight = draw_head_weight(jax.random.fold_in(splits[9], 71), part)
    vocab_blocks = draw_vocab_blocks(jax.random.fold_in(jax.random.fold_in(splits[9], part), 71), part)
    languages = plant(jax.random.randint(part_splits[6], (MB, N_DP, SEQ), 0, LANGS), jax.random.fold_in(part_splits[6], 1), 0, LANGS - 1).astype(jnp.int32)
    targets = plant(jax.random.randint(part_splits[7], (MB, N_DP, SEQ), 0, SEL * BLOCK), jax.random.fold_in(part_splits[7], 1), 0, (SEL * BLOCK) - 1).astype(jnp.int32)
    teacher = jnp.clip(jnp.exp(math.log(0.0078125) - 5.996605 * jax.random.uniform(part_splits[8], (MB, N_DP, SEQ, SEL * BLOCK), jnp.float32) ** levels(part_splits[8], (MB, N_DP, SEQ, SEL * BLOCK), ((1, 4),), -0.2, 0.2)), 1.9431114196777344e-05, 0.0078125).astype(jnp.bfloat16)
    return dict(layer_input=layer_input, attn_gain=attn_gain, qkv_weight=qkv_weight, final_gain=final_gain, head_weight=head_weight, vocab_blocks=vocab_blocks, languages=languages, targets=targets, teacher=teacher)


EPSILON = 1e-06
NEG_FILL = -1e+30

def rms_scaled(values, norm_gain):
    mean_sq = lax.optimization_barrier(jnp.mean(values * values, axis=-1, keepdims=True))
    return values * lax.rsqrt(mean_sq + EPSILON) * norm_gain

def section(residual, norm_gain, weight):
    batch_size, length, feature_width = residual.shape
    widened = residual.astype(jnp.float32)
    normed = rms_scaled(widened, norm_gain).astype(jnp.bfloat16)
    projected = jnp.dot(normed.reshape(batch_size * length, feature_width), weight, preferred_element_type=jnp.float32)
    projected = projected.astype(jnp.bfloat16).reshape(batch_size, length, -1)
    groups = QHEADS // KVHEADS
    queries = projected[:, :, :QHEADS * HEAD].reshape(batch_size, length, KVHEADS, groups, HEAD)
    key_rows = projected[:, :, QHEADS * HEAD:QHEADS * HEAD + KVHEADS * HEAD].reshape(batch_size, length, KVHEADS, HEAD)
    value_rows = projected[:, :, QHEADS * HEAD + KVHEADS * HEAD:].reshape(batch_size, length, KVHEADS, HEAD)
    scores = jnp.einsum('bqhgd,bkhd->bhgqk', queries.astype(jnp.float32), key_rows.astype(jnp.float32)) * HEAD ** (-0.5)
    positions = jnp.arange(length, dtype=jnp.int32)
    causal = positions[:, None] >= positions[None, :]
    scores = jnp.where(causal, scores, NEG_FILL)
    row_max = lax.optimization_barrier(jnp.max(scores, axis=-1, keepdims=True))
    expanded = jnp.exp(scores - row_max)
    weights = (expanded / lax.optimization_barrier(jnp.sum(expanded, axis=-1, keepdims=True))).astype(jnp.bfloat16)
    attended = jnp.einsum('bhgqk,bkhd->bqhgd', weights.astype(jnp.float32), value_rows.astype(jnp.float32))
    attended = attended.reshape(batch_size, length, QHEADS * HEAD)
    return (widened + attended).astype(jnp.bfloat16)

def reference(layer_input, attn_gain, qkv_weight, final_gain, head_weight, vocab_blocks, languages, targets, teacher):
    flat_input = layer_input.reshape(MB * N_DP, SEQ, D)

    def layer_step(state, params):
        return (section(state, params[0], params[1]), None)
    last_layer, _ = lax.scan(layer_step, flat_input, (attn_gain, qkv_weight))
    hidden = rms_scaled(last_layer.astype(jnp.float32), final_gain).astype(jnp.bfloat16)
    hidden = hidden.reshape(MB, N_DP * SEQ, D)
    column_ids = (vocab_blocks[..., None] * BLOCK + jnp.arange(BLOCK, dtype=jnp.int32)).astype(jnp.int32)
    column_ids = column_ids.reshape(MB, LANGS, SEL * BLOCK)
    token_langs = languages.reshape(MB, N_DP * SEQ)

    def per_batch(batch_items):
        row_block, id_rows, lang_row = batch_items

        def per_lang(id_row):
            chosen = jnp.take(head_weight, id_row, axis=1)
            return jnp.dot(row_block, chosen, preferred_element_type=jnp.float32)
        every_lang = lax.map(per_lang, id_rows)
        lang_pick = lang_row[None, :] == jnp.arange(LANGS, dtype=jnp.int32)[:, None]
        return lax.optimization_barrier(jnp.sum(jnp.where(lang_pick[..., None], every_lang, 0.0), axis=0))
    logits = lax.map(per_batch, (hidden, column_ids, token_langs))
    row_max = lax.optimization_barrier(jnp.max(logits, axis=-1))
    row_total = lax.optimization_barrier(jnp.sum(jnp.exp(logits - row_max[..., None]), axis=-1))
    log_total = row_max + jnp.log(row_total)
    teacher_probs = teacher.reshape(MB, N_DP * SEQ, SEL * BLOCK).astype(jnp.float32)
    cross_sum = lax.optimization_barrier(jnp.sum(teacher_probs * logits, axis=-1))
    self_sum = lax.optimization_barrier(jnp.sum(teacher_probs * jnp.log(teacher_probs), axis=-1))
    prob_sum = lax.optimization_barrier(jnp.sum(teacher_probs, axis=-1))
    target_ids = targets.reshape(MB, N_DP * SEQ, 1).astype(jnp.int32)
    target_logit = jnp.take_along_axis(logits, target_ids, axis=-1)[..., 0]
    kl_loss = self_sum - cross_sum + prob_sum * log_total
    ce_loss = log_total - target_logit
    return (kl_loss.reshape(MB, N_DP, SEQ), ce_loss.reshape(MB, N_DP, SEQ))
```

```python
import functools
import jax
import jax.numpy as jnp
from jax import lax
from jax.experimental import pallas as pl
from jax.experimental.pallas import tpu as pltpu
from jax.sharding import PartitionSpec as P

HEAD = 128
QHEADS = 20
KVHEADS = 4
BLOCK = 128
VB_SEGMENT = 20
CAP = 2
GROUP = QHEADS // KVHEADS

EPSILON = 1e-06
NEG_FILL = -1e30

CHUNK = 2
HOP = 2
UNROLL_LIMIT = 32


def section_kernel(seq_len, first_ref, fresh_ref, incoming_ref, gain_ref, wq_ref, wk_ref, wv_ref, out_ref, normed_ref):
    g = pl.program_id(0)
    is_first = first_ref[0] == 1
    tokens = fresh_ref.shape[0]

    @pl.when(g == 0)
    def _():
        rows = jnp.where(is_first, fresh_ref[...].astype(jnp.float32), incoming_ref[...].astype(jnp.float32))
        mean_sq = jnp.mean(rows * rows, axis=-1, keepdims=True)
        normed_ref[...] = (rows * lax.rsqrt(mean_sq + EPSILON) * gain_ref[...]).astype(jnp.bfloat16)

    normed = normed_ref[...]
    q = jnp.dot(normed, wq_ref[...], preferred_element_type=jnp.float32).astype(jnp.bfloat16)
    k = jnp.dot(normed, wk_ref[...], preferred_element_type=jnp.float32).astype(jnp.bfloat16)
    v = jnp.dot(normed, wv_ref[...], preferred_element_type=jnp.float32).astype(jnp.bfloat16)
    stacked = jnp.concatenate([q[:, h * HEAD : (h + 1) * HEAD] for h in range(GROUP)], axis=0)
    scores = lax.dot_general(stacked, k, (((1,), (1,)), ((), ())), preferred_element_type=jnp.float32)
    scores = scores * HEAD ** (-0.5)
    row_at = lax.rem(lax.broadcasted_iota(jnp.int32, scores.shape, 0), tokens)
    col_at = lax.broadcasted_iota(jnp.int32, scores.shape, 1)
    seen = (row_at >= col_at) & (lax.div(row_at, seq_len) == lax.div(col_at, seq_len))
    scores = jnp.where(seen, scores, NEG_FILL)
    row_max = jnp.max(scores, axis=-1, keepdims=True)
    expanded = jnp.exp(scores - row_max)
    probs = (expanded / jnp.sum(expanded, axis=-1, keepdims=True)).astype(jnp.bfloat16)
    attended = jnp.dot(probs, v, preferred_element_type=jnp.float32)
    for h in range(GROUP):
        cols = pl.ds(pl.multiple_of(g * (GROUP * HEAD) + h * HEAD, HEAD), HEAD)
        held = jnp.where(
            is_first, fresh_ref[:, cols].astype(jnp.float32), incoming_ref[:, cols].astype(jnp.float32)
        )
        out_ref[:, h * HEAD : (h + 1) * HEAD] = (held + attended[h * tokens : (h + 1) * tokens]).astype(jnp.bfloat16)


def section(first, fresh, incoming, gain, weight, seq_len):
    tokens, width = fresh.shape
    qw = GROUP * HEAD
    whole = pl.BlockSpec((tokens, width), lambda g, f: (0, 0))
    return pl.pallas_call(
        functools.partial(section_kernel, seq_len),
        out_shape=jax.ShapeDtypeStruct((tokens, width), jnp.bfloat16),
        grid_spec=pltpu.PrefetchScalarGridSpec(
            num_scalar_prefetch=1,
            grid=(KVHEADS,),
            in_specs=[
                whole,
                whole,
                pl.BlockSpec((1, width), lambda g, f: (0, 0)),
                pl.BlockSpec((width, qw), lambda g, f: (0, g)),
                pl.BlockSpec((width, HEAD), lambda g, f: (0, QHEADS + g)),
                pl.BlockSpec((width, HEAD), lambda g, f: (0, QHEADS + KVHEADS + g)),
            ],
            out_specs=pl.BlockSpec((tokens, qw), lambda g, f: (0, g)),
            scratch_shapes=[pltpu.VMEM((tokens, width), jnp.bfloat16)],
        ),
        compiler_params=pltpu.CompilerParams(vmem_limit_bytes=30 * 1024 * 1024),
        cost_estimate=pl.CostEstimate(
            flops=2 * tokens * weight.shape[0] * weight.shape[1],
            bytes_accessed=weight.size * 2 + 3 * tokens * width * 2,
            transcendentals=0,
        ),
        name="section",
    )(first, fresh, incoming, gain, weight, weight, weight)


def head_kernel(
    sources, per_source, local_ref, pos_ref, valid_ref, at_ref, *refs
):
    rows_refs = refs[: sources]
    gain_ref, lang_ref, target_ref, teacher_ref = refs[sources : sources + 4]
    block_refs = refs[sources + 4 : -1]
    out_ref = refs[-1]
    m = pl.program_id(0)
    slots = len(block_refs)
    picked = rows_refs[0][0].astype(jnp.float32)
    for i in range(1, sources):
        picked = jnp.where(at_ref[0] == i, rows_refs[i][0].astype(jnp.float32), picked)
    mean_sq = jnp.mean(picked * picked, axis=-1, keepdims=True)
    hidden = (picked * lax.rsqrt(mean_sq + EPSILON) * gain_ref[...]).astype(jnp.bfloat16)
    lang = lang_ref[0]
    target = target_ref[0]
    every = [jnp.dot(hidden, block_refs[i][...], preferred_element_type=jnp.float32) for i in range(slots)]
    shape = every[0].shape
    lane = lax.broadcasted_iota(jnp.int32, shape, 1)
    langs = slots // CAP
    kept = []
    for c in range(CAP):
        logits = jnp.zeros(shape, jnp.float32)
        probs = jnp.zeros(shape, jnp.float32)
        valid = jnp.zeros(lang.shape, jnp.int32)
        pos = jnp.zeros(lang.shape, jnp.int32)
        for l in range(langs):
            at = m * slots + l * CAP + c
            here = lang == l
            slot_pos = pos_ref[at]
            cols = pl.ds(pl.multiple_of(slot_pos * BLOCK, BLOCK), BLOCK)
            logits = jnp.where(here, every[l * CAP + c], logits)
            probs = jnp.where(here, teacher_ref[0, :, cols].astype(jnp.float32), probs)
            valid = jnp.where(here, valid_ref[at], valid)
            pos = jnp.where(here, slot_pos, pos)
        kept.append((logits, probs, valid == 1, pos))
    row_max = functools.reduce(
        jnp.maximum,
        [jnp.max(jnp.where(v, x, NEG_FILL), axis=-1, keepdims=True) for x, _, v, _ in kept],
    )
    total = jnp.zeros_like(row_max)
    cross = jnp.zeros_like(row_max)
    hit_sum = jnp.zeros_like(row_max)
    for x, p, v, pos in kept:
        total += jnp.sum(jnp.where(v, jnp.exp(jnp.where(v, x, NEG_FILL) - row_max), 0.0), axis=-1, keepdims=True)
        cross += jnp.sum(jnp.where(v, p * x, 0.0), axis=-1, keepdims=True)
        hit = v & (pos * BLOCK + lane == target)
        hit_sum += jnp.sum(jnp.where(hit, x, 0.0), axis=-1, keepdims=True)
    teach = teacher_ref[0].astype(jnp.float32)
    self_sum = jnp.sum(teach * jnp.log(teach), axis=-1, keepdims=True)
    prob_sum = jnp.sum(teach, axis=-1, keepdims=True)
    packed = jnp.zeros(shape, jnp.float32)
    for i, value in enumerate((row_max, total, cross, hit_sum, self_sum, prob_sum)):
        packed = jnp.where(lane == i, value, packed)
    out_ref[0] = packed.T[:8]


def head_stats(at, candidates, final_gain, langs_col, targets_col, teacher, head, local, pos, valid):
    batches, length, width = candidates[0].shape
    slots = local.shape[0] // batches
    sources = len(candidates)

    def block_spec(i):
        return pl.BlockSpec((width, BLOCK), lambda m, lo, po, va, a: (0, lo[m * slots + i]))

    per_batch = lambda *tail: pl.BlockSpec((1,) + tail, lambda m, lo, po, va, a: (m, 0, 0))
    return pl.pallas_call(
        functools.partial(head_kernel, sources, batches),
        out_shape=jax.ShapeDtypeStruct((batches, 8, length), jnp.float32),
        grid_spec=pltpu.PrefetchScalarGridSpec(
            num_scalar_prefetch=4,
            grid=(batches,),
            in_specs=[per_batch(length, width) for _ in range(sources)]
            + [
                pl.BlockSpec((1, width), lambda m, lo, po, va, a: (0, 0)),
                per_batch(length, 1),
                per_batch(length, 1),
                per_batch(length, teacher.shape[-1]),
            ]
            + [block_spec(i) for i in range(slots)],
            out_specs=per_batch(8, length),
        ),
        compiler_params=pltpu.CompilerParams(vmem_limit_bytes=30 * 1024 * 1024),
        cost_estimate=pl.CostEstimate(
            flops=2 * batches * length * width * slots * BLOCK,
            bytes_accessed=batches * width * slots * BLOCK * 2,
            transcendentals=0,
        ),
        name="head_stats",
    )(local, pos, valid, at, *candidates, final_gain, langs_col, targets_col, teacher, *([head] * slots))


def join_kernel(stats_ref, kl_ref, ce_ref):
    count = stats_ref.shape[0]
    stats = [stats_ref[s] for s in range(count)]
    row_max = functools.reduce(jnp.maximum, [s[:, 0, :] for s in stats])
    total = sum(s[:, 1, :] * jnp.exp(s[:, 0, :] - row_max) for s in stats)
    cross = sum(s[:, 2, :] for s in stats)
    hit = sum(s[:, 3, :] for s in stats)
    log_total = row_max + jnp.log(total)
    kl_ref[...] = stats[0][:, 4, :] - cross + stats[0][:, 5, :] * log_total
    ce_ref[...] = log_total - hit


def joined(stats):
    out = jax.ShapeDtypeStruct((stats.shape[1], stats.shape[3]), jnp.float32)
    return pl.pallas_call(join_kernel, out_shape=(out, out), name="join")(stats)


def shifted(value, axis, step, first, last):
    return lax.ppermute(value, axis, [(s, s + step) for s in range(first, last)])


def on_device(
    layer_input,
    attn_gain,
    qkv_weight,
    final_gain,
    head_weight,
    vocab_blocks,
    languages,
    targets,
    teacher,
):
    seg = lax.axis_index("segment")
    count = lax.axis_size("segment")
    batches, _, length, width = layer_input.shape
    chunk = CHUNK if batches % CHUNK == 0 else 1
    chunks = batches // chunk
    tokens = chunk * length
    weight = lax.all_gather(qkv_weight[0], "dp", axis=0, tiled=True)
    head_in, _ = lax.optimization_barrier((head_weight, weight))
    head = lax.all_gather(head_in, "dp", axis=0, tiled=True)
    fresh = layer_input.reshape(chunks, tokens, width)
    gain = attn_gain
    first = (seg == 0).astype(jnp.int32).reshape(1)

    langs = vocab_blocks.shape[1]
    list_len = vocab_blocks.shape[2]
    owned = vocab_blocks // VB_SEGMENT == seg
    order = jnp.cumsum(owned.astype(jnp.int32), axis=-1) - 1
    slot_ids = jnp.arange(CAP, dtype=jnp.int32)
    slot_hit = owned[:, :, None, :] & (order[:, :, None, :] == slot_ids[None, None, :, None])
    valid = jnp.any(slot_hit, axis=-1).astype(jnp.int32).reshape(-1)
    pos = jnp.sum(jnp.where(slot_hit, jnp.arange(list_len, dtype=jnp.int32), 0), axis=-1).reshape(-1)
    local = jnp.sum(jnp.where(slot_hit, vocab_blocks[:, :, None, :] % VB_SEGMENT, 0), axis=-1).reshape(-1)

    steps = chunks + HOP * (count - 1)
    zeros = jnp.zeros((tokens, width), jnp.bfloat16)
    if steps + count <= UNROLL_LIMIT:
        arrived = [zeros] * HOP
        results = []
        for t in range(steps):
            rows = section(first, fresh[min(t, chunks - 1)], arrived[t], gain, weight, length)
            results.append(rows)
            arrived.append(shifted(rows, "segment", 1, 0, count - 1) if t + HOP < steps else zeros)
        hops = [results[steps - chunks :]]
        for j in range(1, count):
            src = count - j
            hops.append([shifted(rows, "segment", -1, src, src + 1) for rows in hops[-1]])
        hops = [jnp.stack(h).reshape(batches, length, width) for h in hops]
        at = (count - 1 - seg).astype(jnp.int32).reshape(1)
    else:
        def turn(t, state):
            incoming, kept = state
            rows = section(first, fresh[jnp.minimum(t, chunks - 1)], incoming, gain, weight, length)
            kept = lax.dynamic_update_index_in_dim(kept, rows, jnp.clip(t - (count - 1), 0, chunks - 1), 0)
            return shifted(rows, "segment", 1, 0, count - 1), kept

        _, kept = lax.fori_loop(
            0, chunks + count - 1, turn, (zeros, jnp.zeros((chunks, tokens, width), jnp.bfloat16))
        )

        def back(j, value):
            moved = shifted(value, "segment", -1, 1, count)
            return jnp.where(seg == count - 1 - j, moved, value)

        kept = lax.fori_loop(1, count, back, kept)
        hops = [kept.reshape(batches, length, width)]
        at = jnp.zeros((1,), jnp.int32)
    stats = head_stats(
        at,
        hops,
        final_gain.reshape(1, width),
        languages.reshape(batches, length, 1),
        targets.reshape(batches, length, 1),
        teacher[:, 0],
        head,
        local,
        pos,
        valid,
    )
    kl, ce = joined(lax.all_gather(stats, "segment"))
    return kl[:, None], ce[:, None]


def solution(mesh):
    return jax.shard_map(
        on_device,
        mesh=mesh,
        in_specs=(
            P("groups", "dp", None, None),
            P("segment", None),
            P("segment", "dp", None),
            P(),
            P("dp", "segment"),
            P("groups", None, None),
            P("groups", "dp", None),
            P("groups", "dp", None),
            P("groups", "dp", None, None),
        ),
        out_specs=(P("groups", "dp", None), P("groups", "dp", None)),
        check_vma=False,
    )
```

```python
import functools
import jax
import jax.numpy as jnp
from jax import lax
from jax.experimental import pallas as pl
from jax.experimental.pallas import tpu as pltpu
from jax.sharding import PartitionSpec as P

HEAD = 128
QHEADS = 20
KVHEADS = 4
BLOCK = 128
VB_SEGMENT = 20
CAP = 2
GROUP = QHEADS // KVHEADS

EPSILON = 1e-06
NEG_FILL = -1e30

CHUNK = 2
HOP = 2
UNROLL_LIMIT = 32
PIECES = (5, 5, 4)
TILE = 896
MIB = 1024 * 1024

WHOLE = pl.BlockSpec(memory_space=pltpu.VMEM)
SCALARS = pl.BlockSpec(memory_space=pltpu.SMEM)


def assemble_kernel(sizes, base_sign, scalar_ref, shard_ref, beside_ref, *refs):
    out_ref, sems = refs[-2:]
    pieces = refs[:-2]
    depth = shard_ref.shape[0]
    half = out_ref.shape[1]
    group, replica = scalar_ref[1], scalar_ref[2]
    side = group if base_sign == 0 else 1 - group
    cols = pl.ds(pl.multiple_of(side * half, HEAD), half)
    rows = [pl.ds(pl.multiple_of(lax.bitwise_xor(replica, j) * depth, HEAD), depth) for j in range(4)]
    copies = [
        pltpu.make_async_copy(shard_ref.at[:, cols], out_ref.at[rows[0], :], sems.at[0]),
        pltpu.make_async_copy(beside_ref.at[:, cols], out_ref.at[rows[1], :], sems.at[1]),
    ]
    offset = 0
    for i, size in enumerate(sizes):
        for j in range(2):
            copies.append(
                pltpu.make_async_copy(
                    pieces[2 * i + j], out_ref.at[rows[2 + j], pl.ds(offset, size)], sems.at[2 + 2 * i + j]
                )
            )
        offset += size
    for copy in copies:
        copy.start()
    for copy in copies:
        copy.wait()


def assembled(base_sign, where, shard, beside, pieces):
    depth, columns = shard.shape
    anywhere = pl.BlockSpec(memory_space=pl.ANY)
    sizes = [p.shape[1] for p in pieces[::2]]
    return pl.pallas_call(
        functools.partial(assemble_kernel, sizes, base_sign),
        out_shape=jax.ShapeDtypeStruct((4 * depth, columns // 2), shard.dtype),
        in_specs=[SCALARS] + [anywhere] * (2 + len(pieces)),
        out_specs=WHOLE,
        scratch_shapes=[pltpu.SemaphoreType.DMA((2 + len(pieces),))],
        compiler_params=pltpu.CompilerParams(vmem_limit_bytes=12 * MIB),
        name="assembled",
    )(where, shard, beside, *pieces)


def gathered_weight(shard, where):
    axes = ("groups", "dp")
    groups, dp = lax.axis_size("groups"), lax.axis_size("dp")
    near = [(g * dp + d, g * dp + (d ^ 1)) for g in range(groups) for d in range(dp)]
    across = [(g * dp + d, g * dp + (d ^ 2)) for g in range(groups) for d in range(dp)]
    other = [(g * dp + d, (1 - g) * dp + d) for g in range(groups) for d in range(dp)]
    rows, columns = shard.shape
    base = lax.axis_index("groups") * (columns // 2)
    beside = lax.ppermute(shard, axes, near)
    offset = 0
    crossed, swapped = [], []
    own_half, swapped_half = [], []
    for i, units in enumerate(PIECES):
        size = units * HEAD
        piece = lax.dynamic_slice(shard, (0, base + offset), (rows, size))
        waits = []
        if i >= 1:
            waits.append(crossed[i - 1])
        if i >= 2:
            waits += [swapped[i - 2], own_half[2 * i - 3]]
        if i >= 3:
            waits.append(swapped_half[2 * i - 5])
        if waits:
            piece = lax.optimization_barrier((piece, *waits))[0]
        crossed.append(lax.ppermute(piece, axes, across))
        swapped.append(lax.ppermute(crossed[i], axes, other))
        own_half += [crossed[i], lax.ppermute(crossed[i], axes, near)]
        swapped_half += [swapped[i], lax.ppermute(swapped[i], axes, near)]
        offset += size
    weights = [
        assembled(0, where, shard, beside, own_half),
        assembled(1, where, shard, beside, swapped_half),
    ]
    return weights, crossed[-1]


def section_kernel(seq_len, after, where_ref, fresh_ref, incoming_ref, gain_ref, *refs):
    weight_refs = refs[after:-2]
    out_ref, proj_ref = refs[-2:]
    is_first = where_ref[0] == 1
    group = where_ref[1]
    tokens = fresh_ref.shape[0]
    half = weight_refs[0].shape[1]

    rows = jnp.where(is_first, fresh_ref[...].astype(jnp.float32), incoming_ref[...].astype(jnp.float32))
    mean_sq = jnp.mean(rows * rows, axis=-1, keepdims=True)
    normed = (rows * lax.rsqrt(mean_sq + EPSILON) * gain_ref[...]).astype(jnp.bfloat16)
    for part, weight_ref in enumerate(weight_refs):
        base = (group if part == 0 else 1 - group) * half
        for low in range(0, half, TILE):
            step = min(TILE, half - low)
            cols = pl.ds(pl.multiple_of(base + low, HEAD), step)
            proj_ref[:, cols] = jnp.dot(
                normed, weight_ref[:, low : low + step], preferred_element_type=jnp.float32
            ).astype(jnp.bfloat16)

    shape = (GROUP * tokens, tokens)
    row_at = lax.rem(lax.broadcasted_iota(jnp.int32, shape, 0), tokens)
    col_at = lax.broadcasted_iota(jnp.int32, shape, 1)
    seen = (row_at >= col_at) & (lax.div(row_at, seq_len) == lax.div(col_at, seq_len))
    for g in range(KVHEADS):
        heads = [slice((g * GROUP + h) * HEAD, (g * GROUP + h + 1) * HEAD) for h in range(GROUP)]
        q = jnp.concatenate([proj_ref[:, cols] for cols in heads], axis=0)
        k = proj_ref[:, (QHEADS + g) * HEAD : (QHEADS + g + 1) * HEAD]
        v = proj_ref[:, (QHEADS + KVHEADS + g) * HEAD : (QHEADS + KVHEADS + g + 1) * HEAD]
        scores = lax.dot_general(q, k, (((1,), (1,)), ((), ())), preferred_element_type=jnp.float32)
        scores = jnp.where(seen, scores * HEAD ** (-0.5), NEG_FILL)
        expanded = jnp.exp(scores - jnp.max(scores, axis=-1, keepdims=True))
        probs = (expanded / jnp.sum(expanded, axis=-1, keepdims=True)).astype(jnp.bfloat16)
        attended = jnp.dot(probs, v, preferred_element_type=jnp.float32)
        for h, cols in enumerate(heads):
            held = jnp.where(
                is_first, fresh_ref[:, cols].astype(jnp.float32), incoming_ref[:, cols].astype(jnp.float32)
            )
            out_ref[:, cols] = (held + attended[h * tokens : (h + 1) * tokens]).astype(jnp.bfloat16)


def section(where, fresh, incoming, gain, weights, seq_len, after=()):
    tokens, width = fresh.shape
    columns = 2 * weights[0].shape[1]
    return pl.pallas_call(
        functools.partial(section_kernel, seq_len, len(after)),
        out_shape=jax.ShapeDtypeStruct((tokens, width), jnp.bfloat16),
        in_specs=[SCALARS] + [WHOLE] * 3 + [pl.BlockSpec(memory_space=pl.ANY)] * len(after) + [WHOLE] * len(weights),
        out_specs=WHOLE,
        scratch_shapes=[
            pltpu.VMEM((tokens, columns), jnp.bfloat16),
        ],
        compiler_params=pltpu.CompilerParams(vmem_limit_bytes=12 * MIB),
        cost_estimate=pl.CostEstimate(
            flops=2 * tokens * width * columns, bytes_accessed=width * columns * 2, transcendentals=0
        ),
        name="section",
    )(where, fresh, incoming, gain, *after, *weights)


def head_kernel(
    first_batch,
    length,
    sources,
    local_ref,
    pos_ref,
    valid_ref,
    at_ref,
    gain_ref,
    lang_ref,
    target_ref,
    teacher_ref,
    head_ref,
    *refs,
):
    source_refs = refs[:sources]
    out_ref = refs[-1]
    earlier = out_ref.shape[0] - 8
    if earlier:
        out_ref[:earlier] = refs[sources][...]
    tokens, width = source_refs[0].shape
    batches = tokens // length
    slots = local_ref.shape[0] // (lang_ref.shape[0] // length)
    langs = slots // CAP
    picked = source_refs[0][...].astype(jnp.float32)
    for i in range(1, sources):
        picked = jnp.where(at_ref[0] == i, source_refs[i][...].astype(jnp.float32), picked)
    mean_sq = jnp.mean(picked * picked, axis=-1, keepdims=True)
    hidden = (picked * lax.rsqrt(mean_sq + EPSILON) * gain_ref[...]).astype(jnp.bfloat16)
    shape = (length, BLOCK)
    lane = lax.broadcasted_iota(jnp.int32, shape, 1)
    for b in range(batches):
        m = first_batch + b
        rows = slice(m * length, (m + 1) * length)
        lang = lang_ref[rows]
        target = target_ref[rows]
        block = jnp.concatenate(
            [
                head_ref[:, pl.ds(pl.multiple_of(local_ref[m * slots + i] * BLOCK, BLOCK), BLOCK)]
                for i in range(slots)
            ],
            axis=1,
        )
        every = jnp.dot(hidden[b * length : (b + 1) * length], block, preferred_element_type=jnp.float32)
        kept = []
        for c in range(CAP):
            logits = jnp.zeros(shape, jnp.float32)
            probs = jnp.zeros(shape, jnp.float32)
            valid = jnp.zeros(lang.shape, jnp.int32)
            pos = jnp.zeros(lang.shape, jnp.int32)
            for l in range(langs):
                at = l * CAP + c
                here = lang == l
                slot_pos = pos_ref[m * slots + at]
                cols = pl.ds(pl.multiple_of(slot_pos * BLOCK, BLOCK), BLOCK)
                logits = jnp.where(here, every[:, at * BLOCK : (at + 1) * BLOCK], logits)
                probs = jnp.where(here, teacher_ref[rows, cols].astype(jnp.float32), probs)
                valid = jnp.where(here, valid_ref[m * slots + at], valid)
                pos = jnp.where(here, slot_pos, pos)
            kept.append((logits, probs, valid == 1, pos))
        row_max = functools.reduce(
            jnp.maximum,
            [jnp.max(jnp.where(v, x, NEG_FILL), axis=-1, keepdims=True) for x, _, v, _ in kept],
        )
        total = jnp.zeros_like(row_max)
        cross = jnp.zeros_like(row_max)
        hit_sum = jnp.zeros_like(row_max)
        for x, p, v, pos in kept:
            total += jnp.sum(jnp.where(v, jnp.exp(jnp.where(v, x, NEG_FILL) - row_max), 0.0), axis=-1, keepdims=True)
            cross += jnp.sum(jnp.where(v, p * x, 0.0), axis=-1, keepdims=True)
            hit = v & (pos * BLOCK + lane == target)
            hit_sum += jnp.sum(jnp.where(hit, x, 0.0), axis=-1, keepdims=True)
        teach = teacher_ref[rows].astype(jnp.float32)
        self_sum = jnp.sum(teach * jnp.log(teach), axis=-1, keepdims=True)
        prob_sum = jnp.sum(teach, axis=-1, keepdims=True)
        packed = jnp.zeros(shape, jnp.float32)
        for i, value in enumerate((row_max, total, cross, hit_sum, self_sum, prob_sum)):
            packed = jnp.where(lane == i, value, packed)
        out_ref[earlier:, b * length : (b + 1) * length] = packed.T[:8]


def head_stats(first_batch, length, scalars, gain, langs_col, targets_col, teacher, head, sources, earlier):
    tokens, width = sources[0].shape
    slots = scalars[0].shape[0] * length // langs_col.shape[0]
    more = [] if earlier is None else [earlier]
    rows = 8 + (0 if earlier is None else earlier.shape[0])
    flops = 2 * tokens * width * slots * BLOCK
    return pl.pallas_call(
        functools.partial(head_kernel, first_batch, length, len(sources)),
        out_shape=jax.ShapeDtypeStruct((rows, tokens), jnp.float32),
        in_specs=[SCALARS] * 4 + [WHOLE] * (5 + len(sources) + len(more)),
        out_specs=WHOLE,
        compiler_params=pltpu.CompilerParams(vmem_limit_bytes=12 * MIB),
        cost_estimate=pl.CostEstimate(flops=flops, bytes_accessed=4 * MIB, transcendentals=0),
        name="head_stats",
    )(*scalars, gain, langs_col, targets_col, teacher, head, *sources, *more)


def join_kernel(length, *refs):
    stats_refs = refs[:-2]
    kl_ref, ce_ref = refs[-2:]
    tokens = stats_refs[0].shape[1]
    per_chunk = tokens // length
    for k in range(stats_refs[0].shape[0] // 8):
        stats = [ref[8 * k : 8 * k + 8, :] for ref in stats_refs]
        row_max = functools.reduce(jnp.maximum, [s[0:1] for s in stats])
        total = sum(s[1:2] * jnp.exp(s[0:1] - row_max) for s in stats)
        cross = sum(s[2:3] for s in stats)
        hit = sum(s[3:4] for s in stats)
        log_total = row_max + jnp.log(total)
        kl = stats[0][4:5] - cross + stats[0][5:6] * log_total
        ce = log_total - hit
        for b in range(per_chunk):
            row = k * per_chunk + b
            kl_ref[row : row + 1] = kl[:, b * length : (b + 1) * length]
            ce_ref[row : row + 1] = ce[:, b * length : (b + 1) * length]


def joined(stats, length):
    rows, tokens = stats[0].shape
    out = jax.ShapeDtypeStruct((rows // 8 * tokens // length, length), jnp.float32)
    return pl.pallas_call(
        functools.partial(join_kernel, length),
        out_shape=(out, out),
        in_specs=[WHOLE] * len(stats),
        out_specs=(WHOLE, WHOLE),
        name="join",
    )(*stats)


def shifted(value, axis, step, first, last):
    return lax.ppermute(value, axis, [(s, s + step) for s in range(first, last)])


def on_device(
    layer_input,
    attn_gain,
    qkv_weight,
    final_gain,
    head_weight,
    vocab_blocks,
    languages,
    targets,
    teacher,
):
    seg = lax.axis_index("segment")
    count = lax.axis_size("segment")
    batches, _, length, width = layer_input.shape
    chunk = CHUNK if batches % CHUNK == 0 else 1
    chunks = batches // chunk
    tokens = chunk * length
    where = jnp.stack(
        [(seg == 0).astype(jnp.int32), lax.axis_index("groups"), lax.axis_index("dp")]
    ).astype(jnp.int32)
    weights, crossed = gathered_weight(qkv_weight[0], where)
    head_in, _ = lax.optimization_barrier((head_weight, crossed))
    head = lax.all_gather(head_in, "dp", axis=0, tiled=True)
    fresh = layer_input.reshape(chunks, tokens, width)

    list_len = vocab_blocks.shape[2]
    owned = vocab_blocks // VB_SEGMENT == seg
    order = jnp.cumsum(owned.astype(jnp.int32), axis=-1) - 1
    slot_ids = jnp.arange(CAP, dtype=jnp.int32)
    slot_hit = owned[:, :, None, :] & (order[:, :, None, :] == slot_ids[None, None, :, None])
    valid = jnp.any(slot_hit, axis=-1).astype(jnp.int32).reshape(-1)
    pos = jnp.sum(jnp.where(slot_hit, jnp.arange(list_len, dtype=jnp.int32), 0), axis=-1).reshape(-1)
    local = jnp.sum(jnp.where(slot_hit, vocab_blocks[:, :, None, :] % VB_SEGMENT, 0), axis=-1).reshape(-1)

    steps = chunks + HOP * (count - 1)
    zeros = jnp.zeros((tokens, width), jnp.bfloat16)
    unrolled = steps + count <= UNROLL_LIMIT
    if unrolled:
        arrived = [zeros] * HOP
        sources = []
        moving = [[] for _ in range(steps + HOP)]
        for t in range(steps):
            rows = section(
                where, fresh[min(t, chunks - 1)], arrived[t], attn_gain, weights, length, [h[-1] for h in moving[t]]
            )
            arrived.append(shifted(rows, "segment", 1, 0, count - 1) if t + HOP < steps else zeros)
            going = moving[t]
            if t >= steps - chunks:
                sources.append([rows])
                going = [sources[-1]] + going
            for hops in going:
                if len(hops) < count:
                    src = count - len(hops)
                    hops.append(shifted(hops[-1], "segment", -1, src, src + 1))
                    moving[t + HOP].append(hops)
        for hops in sources:
            while len(hops) < count:
                src = count - len(hops)
                hops.append(shifted(hops[-1], "segment", -1, src, src + 1))
        at = (count - 1 - seg).astype(jnp.int32).reshape(1)
    else:

        def turn(t, state):
            incoming, kept = state
            now = lax.dynamic_index_in_dim(fresh, jnp.minimum(t, chunks - 1), 0, False)
            rows = section(where, now, incoming, attn_gain, weights, length)
            kept = lax.dynamic_update_index_in_dim(kept, rows, jnp.clip(t - (count - 1), 0, chunks - 1), 0)
            return shifted(rows, "segment", 1, 0, count - 1), kept

        _, kept = lax.fori_loop(
            0, chunks + count - 1, turn, (zeros, jnp.zeros((chunks, tokens, width), jnp.bfloat16))
        )

        def back(j, value):
            moved = shifted(value, "segment", -1, 1, count)
            return jnp.where(seg == count - 1 - j, moved, value)

        kept = lax.fori_loop(1, count, back, kept)
        sources = [[kept[k]] for k in range(chunks)]
        at = jnp.zeros((1,), jnp.int32)

    stats = None
    for k in range(chunks):
        stats = head_stats(
            k * chunk,
            length,
            (local, pos, valid, at),
            final_gain.reshape(1, width),
            languages.reshape(batches * length, 1),
            targets.reshape(batches * length, 1),
            teacher.reshape(batches * length, -1),
            head,
            sources[k],
            stats,
        )
    if unrolled:
        every = [stats] + [
            lax.ppermute(stats, "segment", [(s, (s + j) % count) for s in range(count)])
            for j in range(1, count)
        ]
    else:
        gathered = lax.all_gather(stats, "segment")
        every = [gathered[s] for s in range(count)]
    kl, ce = joined(every, length)
    return kl[:, None], ce[:, None]


def solution(mesh):
    return jax.shard_map(
        on_device,
        mesh=mesh,
        in_specs=(
            P("groups", "dp", None, None),
            P("segment", None),
            P("segment", "dp", None),
            P(),
            P("dp", "segment"),
            P("groups", None, None),
            P("groups", "dp", None),
            P("groups", "dp", None),
            P("groups", "dp", None, None),
        ),
        out_specs=(P("groups", "dp", None), P("groups", "dp", None)),
        check_vma=False,
    )
```

```python
import functools
import jax
import jax.numpy as jnp
from jax import lax
from jax.experimental import pallas as pl
from jax.experimental.pallas import tpu as pltpu
from jax.sharding import PartitionSpec as P

HEAD = 128
QHEADS = 20
KVHEADS = 4
BLOCK = 128
VB_SEGMENT = 20
CAP = 2
GROUP = QHEADS // KVHEADS

EPSILON = 1e-06
NEG_FILL = -1e30

CHUNKS = (2, 2, 2, 2)
HOP = 2
BACK = 2
UNROLL_LIMIT = 32
PIECES = (4, 4, 4, 2)
TILE = 896
MIB = 1024 * 1024

WHOLE = pl.BlockSpec(memory_space=pltpu.VMEM)
SCALARS = pl.BlockSpec(memory_space=pltpu.SMEM)


def assemble_kernel(sizes, base_sign, scalar_ref, shard_ref, beside_ref, *refs):
    out_ref, sems = refs[-2:]
    pieces = refs[:-2]
    depth = shard_ref.shape[0]
    half = out_ref.shape[1]
    group, replica = scalar_ref[1], scalar_ref[2]
    side = group if base_sign == 0 else 1 - group
    cols = pl.ds(pl.multiple_of(side * half, HEAD), half)
    rows = [pl.ds(pl.multiple_of(lax.bitwise_xor(replica, j) * depth, HEAD), depth) for j in range(4)]
    copies = [
        pltpu.make_async_copy(shard_ref.at[:, cols], out_ref.at[rows[0], :], sems.at[0]),
        pltpu.make_async_copy(beside_ref.at[:, cols], out_ref.at[rows[1], :], sems.at[1]),
    ]
    offset = 0
    for i, size in enumerate(sizes):
        for j in range(2):
            copies.append(
                pltpu.make_async_copy(
                    pieces[2 * i + j], out_ref.at[rows[2 + j], pl.ds(offset, size)], sems.at[2 + 2 * i + j]
                )
            )
        offset += size
    for copy in copies:
        copy.start()
    for copy in copies:
        copy.wait()


def assembled(base_sign, where, shard, beside, pieces):
    depth, columns = shard.shape
    anywhere = pl.BlockSpec(memory_space=pl.ANY)
    sizes = [p.shape[1] for p in pieces[::2]]
    return pl.pallas_call(
        functools.partial(assemble_kernel, sizes, base_sign),
        out_shape=jax.ShapeDtypeStruct((4 * depth, columns // 2), shard.dtype),
        in_specs=[SCALARS] + [anywhere] * (2 + len(pieces)),
        out_specs=WHOLE,
        scratch_shapes=[pltpu.SemaphoreType.DMA((2 + len(pieces),))],
        compiler_params=pltpu.CompilerParams(vmem_limit_bytes=12 * MIB),
        name="assembled",
    )(where, shard, beside, *pieces)


def gathered_weight(shard, where):
    axes = ("groups", "dp")
    groups, dp = lax.axis_size("groups"), lax.axis_size("dp")
    near = [(g * dp + d, g * dp + (d ^ 1)) for g in range(groups) for d in range(dp)]
    across = [(g * dp + d, g * dp + (d ^ 2)) for g in range(groups) for d in range(dp)]
    other = [(g * dp + d, (1 - g) * dp + d) for g in range(groups) for d in range(dp)]
    rows, columns = shard.shape
    base = lax.axis_index("groups") * (columns // 2)
    beside = lax.ppermute(shard, axes, near)
    offset = 0
    crossed, swapped = [], []
    own_half, swapped_half, moved_near = [], [], {}
    for i, units in enumerate(PIECES):
        size = units * HEAD
        piece = lax.dynamic_slice(shard, (0, base + offset), (rows, size))
        waits = []
        if i >= 1:
            waits.append(crossed[i - 1])
        if i >= 2:
            waits += [swapped[i - 2], own_half[2 * i - 3]]
        if i >= 3:
            moved_near[i - 3] = lax.ppermute(swapped[i - 3], axes, near)
            waits.append(moved_near[i - 3])
        if waits:
            piece = lax.optimization_barrier((piece, *waits))[0]
        crossed.append(lax.ppermute(piece, axes, across))
        swapped.append(lax.ppermute(crossed[i], axes, other))
        own_half += [crossed[i], lax.ppermute(crossed[i], axes, near)]
        swapped_half.append(swapped[i])
        offset += size
    first_half = assembled(0, where, shard, beside, own_half)
    pairs = []
    for i, value in enumerate(swapped_half):
        passing = value
        if i == len(PIECES) - 2:
            passing, first_half = lax.optimization_barrier((passing, first_half))
        pairs += [value, moved_near[i] if i in moved_near else lax.ppermute(passing, axes, near)]
    weights = [first_half, assembled(1, where, shard, beside, pairs)]
    return weights, crossed[-1]


def section_kernel(seq_len, turn, after, where_ref, fresh_ref, incoming_ref, gain_ref, *refs):
    weight_refs = refs[after:-2]
    out_ref, proj_ref = refs[-2:]
    is_first = where_ref[0] == 1
    group = where_ref[1]
    tokens = incoming_ref.shape[0]
    fresh_rows = pl.ds(where_ref[3] * tokens if turn is None else turn, tokens)
    half = weight_refs[0].shape[1]

    rows = jnp.where(is_first, fresh_ref[fresh_rows].astype(jnp.float32), incoming_ref[...].astype(jnp.float32))
    mean_sq = jnp.mean(rows * rows, axis=-1, keepdims=True)
    normed = (rows * lax.rsqrt(mean_sq + EPSILON) * gain_ref[...]).astype(jnp.bfloat16)
    for part, weight_ref in enumerate(weight_refs):
        base = (group if part == 0 else 1 - group) * half
        for low in range(0, half, TILE):
            step = min(TILE, half - low)
            cols = pl.ds(pl.multiple_of(base + low, HEAD), step)
            proj_ref[:, cols] = jnp.dot(
                normed, weight_ref[:, low : low + step], preferred_element_type=jnp.float32
            ).astype(jnp.bfloat16)

    shape = (GROUP * tokens, tokens)
    row_at = lax.rem(lax.broadcasted_iota(jnp.int32, shape, 0), tokens)
    col_at = lax.broadcasted_iota(jnp.int32, shape, 1)
    seen = (row_at >= col_at) & (lax.div(row_at, seq_len) == lax.div(col_at, seq_len))
    for g in range(KVHEADS):
        heads = [slice((g * GROUP + h) * HEAD, (g * GROUP + h + 1) * HEAD) for h in range(GROUP)]
        q = jnp.concatenate([proj_ref[:, cols] for cols in heads], axis=0)
        k = proj_ref[:, (QHEADS + g) * HEAD : (QHEADS + g + 1) * HEAD]
        v = proj_ref[:, (QHEADS + KVHEADS + g) * HEAD : (QHEADS + KVHEADS + g + 1) * HEAD]
        scores = lax.dot_general(q, k, (((1,), (1,)), ((), ())), preferred_element_type=jnp.float32)
        scores = jnp.where(seen, scores * HEAD ** (-0.5), NEG_FILL)
        expanded = jnp.exp(scores - jnp.max(scores, axis=-1, keepdims=True))
        probs = (expanded / jnp.sum(expanded, axis=-1, keepdims=True)).astype(jnp.bfloat16)
        attended = jnp.dot(probs, v, preferred_element_type=jnp.float32)
        for h, cols in enumerate(heads):
            held = jnp.where(
                is_first, fresh_ref[fresh_rows, cols].astype(jnp.float32), incoming_ref[:, cols].astype(jnp.float32)
            )
            out_ref[:, cols] = (held + attended[h * tokens : (h + 1) * tokens]).astype(jnp.bfloat16)


def section(where, fresh, turn, incoming, gain, weights, seq_len, after=()):
    tokens, width = incoming.shape
    columns = 2 * weights[0].shape[1]
    return pl.pallas_call(
        functools.partial(section_kernel, seq_len, turn, len(after)),
        out_shape=jax.ShapeDtypeStruct((tokens, width), jnp.bfloat16),
        in_specs=[SCALARS] + [WHOLE] * 3 + [pl.BlockSpec(memory_space=pl.ANY)] * len(after) + [WHOLE] * len(weights),
        out_specs=WHOLE,
        scratch_shapes=[
            pltpu.VMEM((tokens, columns), jnp.bfloat16),
        ],
        compiler_params=pltpu.CompilerParams(vmem_limit_bytes=12 * MIB),
        cost_estimate=pl.CostEstimate(
            flops=2 * tokens * width * columns, bytes_accessed=width * columns * 2, transcendentals=0
        ),
        name="section",
    )(where, fresh, incoming, gain, *after, *weights)


def head_kernel(
    first_batch,
    length,
    sources,
    local_ref,
    pos_ref,
    valid_ref,
    at_ref,
    gain_ref,
    lang_ref,
    target_ref,
    teacher_ref,
    head_ref,
    *refs,
):
    source_refs = refs[:sources]
    out_ref = refs[-1]
    earlier = out_ref.shape[0] - 8
    out_ref[...] = jnp.zeros_like(out_ref)
    if earlier:
        out_ref[:earlier] = refs[sources][...]
    tokens, width = source_refs[0].shape
    batches = tokens // length
    slots = local_ref.shape[0] // (lang_ref.shape[0] // length)
    langs = slots // CAP
    picked = source_refs[0][...].astype(jnp.float32)
    for i in range(1, sources):
        picked = jnp.where(at_ref[0] == i, source_refs[i][...].astype(jnp.float32), picked)
    mean_sq = jnp.mean(picked * picked, axis=-1, keepdims=True)
    hidden = (picked * lax.rsqrt(mean_sq + EPSILON) * gain_ref[...]).astype(jnp.bfloat16)
    shape = (length, BLOCK)
    lane = lax.broadcasted_iota(jnp.int32, shape, 1)
    for b in range(batches):
        m = first_batch + b
        rows = slice(m * length, (m + 1) * length)
        lang = lang_ref[rows]
        target = target_ref[rows]
        block = jnp.concatenate(
            [
                head_ref[:, pl.ds(pl.multiple_of(local_ref[m * slots + i] * BLOCK, BLOCK), BLOCK)]
                for i in range(slots)
            ],
            axis=1,
        )
        every = jnp.dot(hidden[b * length : (b + 1) * length], block, preferred_element_type=jnp.float32)
        kept = []
        for c in range(CAP):
            logits = jnp.zeros(shape, jnp.float32)
            probs = jnp.zeros(shape, jnp.float32)
            valid = jnp.zeros(lang.shape, jnp.int32)
            pos = jnp.zeros(lang.shape, jnp.int32)
            for l in range(langs):
                at = l * CAP + c
                here = lang == l
                slot_pos = pos_ref[m * slots + at]
                cols = pl.ds(pl.multiple_of(slot_pos * BLOCK, BLOCK), BLOCK)
                logits = jnp.where(here, every[:, at * BLOCK : (at + 1) * BLOCK], logits)
                probs = jnp.where(here, teacher_ref[rows, cols].astype(jnp.float32), probs)
                valid = jnp.where(here, valid_ref[m * slots + at], valid)
                pos = jnp.where(here, slot_pos, pos)
            kept.append((logits, probs, valid == 1, pos))
        row_max = functools.reduce(
            jnp.maximum,
            [jnp.max(jnp.where(v, x, NEG_FILL), axis=-1, keepdims=True) for x, _, v, _ in kept],
        )
        total = jnp.zeros_like(row_max)
        cross = jnp.zeros_like(row_max)
        hit_sum = jnp.zeros_like(row_max)
        for x, p, v, pos in kept:
            total += jnp.sum(jnp.where(v, jnp.exp(jnp.where(v, x, NEG_FILL) - row_max), 0.0), axis=-1, keepdims=True)
            cross += jnp.sum(jnp.where(v, p * x, 0.0), axis=-1, keepdims=True)
            hit = v & (pos * BLOCK + lane == target)
            hit_sum += jnp.sum(jnp.where(hit, x, 0.0), axis=-1, keepdims=True)
        teach = teacher_ref[rows].astype(jnp.float32)
        self_sum = jnp.sum(teach * jnp.log(teach), axis=-1, keepdims=True)
        prob_sum = jnp.sum(teach, axis=-1, keepdims=True)
        packed = jnp.zeros(shape, jnp.float32)
        for i, value in enumerate((row_max, total, cross, hit_sum, self_sum, prob_sum)):
            packed = jnp.where(lane == i, value, packed)
        out_ref[earlier:, b * length : (b + 1) * length] = packed.T[:8]


def head_stats(first_batch, lanes, length, scalars, gain, langs_col, targets_col, teacher, head, sources, earlier):
    tokens, width = sources[0].shape
    slots = scalars[0].shape[0] * length // langs_col.shape[0]
    more = [] if earlier is None else [earlier]
    rows = 8 + (0 if earlier is None else earlier.shape[0])
    flops = 2 * tokens * width * slots * BLOCK
    return pl.pallas_call(
        functools.partial(head_kernel, first_batch, length, len(sources)),
        out_shape=jax.ShapeDtypeStruct((rows, lanes), jnp.float32),
        in_specs=[SCALARS] * 4 + [WHOLE] * (5 + len(sources) + len(more)),
        out_specs=WHOLE,
        compiler_params=pltpu.CompilerParams(vmem_limit_bytes=12 * MIB),
        cost_estimate=pl.CostEstimate(flops=flops, bytes_accessed=4 * MIB, transcendentals=0),
        name="head_stats",
    )(*scalars, gain, langs_col, targets_col, teacher, head, *sources, *more)


def join_kernel(length, sizes, *refs):
    stats_refs = refs[:-2]
    kl_ref, ce_ref = refs[-2:]
    row = 0
    for k, size in enumerate(sizes):
        stats = [ref[8 * k : 8 * k + 8, :] for ref in stats_refs]
        row_max = functools.reduce(jnp.maximum, [s[0:1] for s in stats])
        total = sum(s[1:2] * jnp.exp(s[0:1] - row_max) for s in stats)
        cross = sum(s[2:3] for s in stats)
        hit = sum(s[3:4] for s in stats)
        log_total = row_max + jnp.log(total)
        kl = stats[0][4:5] - cross + stats[0][5:6] * log_total
        ce = log_total - hit
        for b in range(size):
            kl_ref[row : row + 1] = kl[:, b * length : (b + 1) * length]
            ce_ref[row : row + 1] = ce[:, b * length : (b + 1) * length]
            row += 1


def joined(stats, length, sizes):
    out = jax.ShapeDtypeStruct((sum(sizes), length), jnp.float32)
    return pl.pallas_call(
        functools.partial(join_kernel, length, sizes),
        out_shape=(out, out),
        in_specs=[WHOLE] * len(stats),
        out_specs=(WHOLE, WHOLE),
        name="join",
    )(*stats)


def shifted(value, axis, step, first, last):
    return lax.ppermute(value, axis, [(s, s + step) for s in range(first, last)])


def on_device(
    layer_input,
    attn_gain,
    qkv_weight,
    final_gain,
    head_weight,
    vocab_blocks,
    languages,
    targets,
    teacher,
):
    seg = lax.axis_index("segment")
    count = lax.axis_size("segment")
    batches, _, length, width = layer_input.shape
    steps = len(CHUNKS) + HOP * (count - 1)
    unrolled = sum(CHUNKS) == batches and steps + count <= UNROLL_LIMIT
    sizes = CHUNKS if unrolled else (1,) * batches
    chunks = len(sizes)
    starts = [sum(sizes[:k]) for k in range(chunks)]
    where = jnp.stack(
        [(seg == 0).astype(jnp.int32), lax.axis_index("groups"), lax.axis_index("dp")]
    ).astype(jnp.int32)
    weights, crossed = gathered_weight(qkv_weight[0], where)
    head_in, _ = lax.optimization_barrier((head_weight, crossed))
    head = lax.all_gather(head_in, "dp", axis=0, tiled=True)
    fresh = layer_input.reshape(batches * length, width)

    list_len = vocab_blocks.shape[2]
    owned = vocab_blocks // VB_SEGMENT == seg
    order = jnp.cumsum(owned.astype(jnp.int32), axis=-1) - 1
    slot_ids = jnp.arange(CAP, dtype=jnp.int32)
    slot_hit = owned[:, :, None, :] & (order[:, :, None, :] == slot_ids[None, None, :, None])
    valid = jnp.any(slot_hit, axis=-1).astype(jnp.int32).reshape(-1)
    pos = jnp.sum(jnp.where(slot_hit, jnp.arange(list_len, dtype=jnp.int32), 0), axis=-1).reshape(-1)
    local = jnp.sum(jnp.where(slot_hit, vocab_blocks[:, :, None, :] % VB_SEGMENT, 0), axis=-1).reshape(-1)

    if unrolled:
        arrived = []
        previous = []
        sources = []
        moving = [[] for _ in range(steps + HOP)]
        for t in range(steps):
            k = min(t, chunks - 1)
            spare = jnp.zeros((sizes[k] * length, width), jnp.bfloat16)
            rows = section(
                where,
                fresh,
                starts[k] * length,
                arrived[t - HOP] if t >= HOP else spare,
                attn_gain,
                weights,
                length,
                previous + [h[-1] for h in moving[t]],
            )
            previous = [rows]
            arrived.append(shifted(rows, "segment", 1, 0, count - 1) if t + HOP < steps else None)
            going = moving[t]
            if t >= steps - chunks:
                sources.append([rows])
                going = [sources[-1]] + going
            for hops in going:
                if len(hops) < count and t < steps - 1:
                    src = count - len(hops)
                    hops.append(shifted(hops[-1], "segment", -1, src, src + 1))
                    moving[t + BACK].append(hops)
        last = sources[-1][0]
        for hops in sources[:-1]:
            while len(hops) < count:
                src = count - len(hops)
                passing, _ = lax.optimization_barrier((hops[-1], last))
                hops.append(shifted(passing, "segment", -1, src, src + 1))
        direct = [
            lax.ppermute(last, "segment", [(count - 1, count - 1 - j)]) for j in range(count - 1, 0, -1)
        ]
        sources[-1] = [last] + direct[::-1]
        at = (count - 1 - seg).astype(jnp.int32).reshape(1)
    else:

        def turn(t, state):
            incoming, kept = state
            here = jnp.concatenate([where, jnp.minimum(t, chunks - 1).astype(jnp.int32).reshape(1)])
            rows = section(here, fresh, None, incoming, attn_gain, weights, length)
            kept = lax.dynamic_update_index_in_dim(kept, rows, jnp.clip(t - (count - 1), 0, chunks - 1), 0)
            return shifted(rows, "segment", 1, 0, count - 1), kept

        zeros = jnp.zeros((length, width), jnp.bfloat16)
        _, kept = lax.fori_loop(
            0, chunks + count - 1, turn, (zeros, jnp.zeros((chunks, length, width), jnp.bfloat16))
        )

        def back(j, value):
            moved = shifted(value, "segment", -1, 1, count)
            return jnp.where(seg == count - 1 - j, moved, value)

        kept = lax.fori_loop(1, count, back, kept)
        sources = [[kept[k]] for k in range(chunks)]
        at = jnp.zeros((1,), jnp.int32)

    stats = None
    for k in range(chunks):
        stats = head_stats(
            starts[k],
            max(sizes) * length,
            length,
            (local, pos, valid, at),
            final_gain.reshape(1, width),
            languages.reshape(batches * length, 1),
            targets.reshape(batches * length, 1),
            teacher.reshape(batches * length, -1),
            head,
            sources[k],
            stats,
        )
    if unrolled:
        every = [stats] + [
            lax.ppermute(stats, "segment", [(s, (s + j) % count) for s in range(count)])
            for j in range(1, count)
        ]
    else:
        gathered = lax.all_gather(stats, "segment")
        every = [gathered[s] for s in range(count)]
    kl, ce = joined(every, length, sizes)
    return kl[:, None], ce[:, None]


def solution(mesh):
    return jax.shard_map(
        on_device,
        mesh=mesh,
        in_specs=(
            P("groups", "dp", None, None),
            P("segment", None),
            P("segment", "dp", None),
            P(),
            P("dp", "segment"),
            P("groups", None, None),
            P("groups", "dp", None),
            P("groups", "dp", None),
            P("groups", "dp", None, None),
        ),
        out_specs=(P("groups", "dp", None), P("groups", "dp", None)),
        check_vma=False,
    )
```

```python
import functools
import jax
import jax.numpy as jnp
from jax import lax
from jax.experimental import pallas as pl
from jax.experimental.pallas import tpu as pltpu
from jax.sharding import PartitionSpec as P

HEAD = 128
QHEADS = 20
KVHEADS = 4
BLOCK = 128
VB_SEGMENT = 20
CAP = 2
GROUP = QHEADS // KVHEADS

EPSILON = 1e-06
NEG_FILL = -1e30

CHUNKS = (2, 2, 2, 2)
HOP = 2
BACK = 2
UNROLL_LIMIT = 32
PIECES = (4, 4, 4)
TILE = 896
MIB = 1024 * 1024

WHOLE = pl.BlockSpec(memory_space=pltpu.VMEM)
SCALARS = pl.BlockSpec(memory_space=pltpu.SMEM)


def assemble_kernel(sizes, base_sign, scalar_ref, shard_ref, beside_ref, *refs):
    out_ref, sems = refs[-2:]
    pieces = refs[:-2]
    depth = shard_ref.shape[0]
    half = out_ref.shape[1]
    group, replica = scalar_ref[1], scalar_ref[2]
    side = group if base_sign == 0 else 1 - group
    cols = pl.ds(pl.multiple_of(side * half, HEAD), half)
    rows = [pl.ds(pl.multiple_of(lax.bitwise_xor(replica, j) * depth, HEAD), depth) for j in range(4)]
    copies = [
        pltpu.make_async_copy(shard_ref.at[:, cols], out_ref.at[rows[0], :], sems.at[0]),
        pltpu.make_async_copy(beside_ref.at[:, cols], out_ref.at[rows[1], :], sems.at[1]),
    ]
    offset = 0
    for i, size in enumerate(sizes):
        for j in range(2):
            copies.append(
                pltpu.make_async_copy(
                    pieces[2 * i + j], out_ref.at[rows[2 + j], pl.ds(offset, size)], sems.at[2 + 2 * i + j]
                )
            )
        offset += size
    for copy in copies:
        copy.start()
    for copy in copies:
        copy.wait()


def assembled(base_sign, where, shard, beside, pieces):
    depth, columns = shard.shape
    anywhere = pl.BlockSpec(memory_space=pl.ANY)
    sizes = [p.shape[1] for p in pieces[::2]]
    return pl.pallas_call(
        functools.partial(assemble_kernel, sizes, base_sign),
        out_shape=jax.ShapeDtypeStruct((4 * depth, columns // 2), shard.dtype),
        in_specs=[SCALARS] + [anywhere] * (2 + len(pieces)),
        out_specs=WHOLE,
        scratch_shapes=[pltpu.SemaphoreType.DMA((2 + len(pieces),))],
        compiler_params=pltpu.CompilerParams(vmem_limit_bytes=12 * MIB),
        name="assembled",
    )(where, shard, beside, *pieces)


def gathered_weight(shard, where):
    axes = ("groups", "dp")
    groups, dp = lax.axis_size("groups"), lax.axis_size("dp")
    near = [(g * dp + d, g * dp + (d ^ 1)) for g in range(groups) for d in range(dp)]
    across = [(g * dp + d, g * dp + (d ^ 2)) for g in range(groups) for d in range(dp)]
    other = [(g * dp + d, (1 - g) * dp + d) for g in range(groups) for d in range(dp)]
    rows, columns = shard.shape
    half = columns // 2
    base = lax.axis_index("groups") * half
    beside = lax.ppermute(shard, axes, near)
    offset = 0
    crossed, swapped = [], []
    own_half, moved_near = [], {}

    def waits_before(i):
        waits = []
        if i >= 1:
            waits.append(crossed[i - 1])
        if i >= 2:
            waits += [swapped[i - 2], own_half[2 * i - 3]]
        if i >= 3:
            moved_near[i - 3] = lax.ppermute(swapped[i - 3], axes, near)
            waits.append(moved_near[i - 3])
        return waits

    for i, units in enumerate(PIECES):
        piece = lax.dynamic_slice(shard, (0, base + offset), (rows, units * HEAD))
        piece = lax.optimization_barrier((piece, *waits_before(i)))[0]
        crossed.append(lax.ppermute(piece, axes, across))
        swapped.append(lax.ppermute(crossed[i], axes, other))
        own_half += [crossed[i], lax.ppermute(crossed[i], axes, near)]
        offset += units * HEAD
    rest = [
        lax.dynamic_slice(shard, (0, at + offset), (rows, half - offset)) for at in (base, half - base)
    ]
    rest = lax.optimization_barrier((*rest, *waits_before(len(PIECES))))[:2]
    rest = [lax.ppermute(piece, axes, across) for piece in rest]
    rest = [(piece, lax.ppermute(piece, axes, near)) for piece in rest]
    first_half = assembled(0, where, shard, beside, own_half + list(rest[0]))
    pairs = []
    for i, value in enumerate(swapped):
        passing = value
        if i == len(PIECES) - 1:
            passing, first_half = lax.optimization_barrier((passing, first_half))
        pairs += [value, moved_near[i] if i in moved_near else lax.ppermute(passing, axes, near)]
    weights = [first_half, assembled(1, where, shard, beside, pairs + list(rest[1]))]
    return weights, rest[1][0]


def section_kernel(seq_len, turn, after, where_ref, fresh_ref, incoming_ref, gain_ref, *refs):
    weight_refs = refs[after:-2]
    out_ref, proj_ref = refs[-2:]
    is_first = where_ref[0] == 1
    group = where_ref[1]
    tokens = incoming_ref.shape[0]
    fresh_rows = pl.ds(where_ref[3] * tokens if turn is None else turn, tokens)
    half = weight_refs[0].shape[1]

    rows = jnp.where(is_first, fresh_ref[fresh_rows].astype(jnp.float32), incoming_ref[...].astype(jnp.float32))
    mean_sq = jnp.mean(rows * rows, axis=-1, keepdims=True)
    normed = (rows * lax.rsqrt(mean_sq + EPSILON) * gain_ref[...]).astype(jnp.bfloat16)
    for part, weight_ref in enumerate(weight_refs):
        base = (group if part == 0 else 1 - group) * half
        for low in range(0, half, TILE):
            step = min(TILE, half - low)
            cols = pl.ds(pl.multiple_of(base + low, HEAD), step)
            proj_ref[:, cols] = jnp.dot(
                normed, weight_ref[:, low : low + step], preferred_element_type=jnp.float32
            ).astype(jnp.bfloat16)

    shape = (GROUP * tokens, tokens)
    row_at = lax.rem(lax.broadcasted_iota(jnp.int32, shape, 0), tokens)
    col_at = lax.broadcasted_iota(jnp.int32, shape, 1)
    seen = (row_at >= col_at) & (lax.div(row_at, seq_len) == lax.div(col_at, seq_len))
    for g in range(KVHEADS):
        heads = [slice((g * GROUP + h) * HEAD, (g * GROUP + h + 1) * HEAD) for h in range(GROUP)]
        q = jnp.concatenate([proj_ref[:, cols] for cols in heads], axis=0)
        k = proj_ref[:, (QHEADS + g) * HEAD : (QHEADS + g + 1) * HEAD]
        v = proj_ref[:, (QHEADS + KVHEADS + g) * HEAD : (QHEADS + KVHEADS + g + 1) * HEAD]
        scores = lax.dot_general(q, k, (((1,), (1,)), ((), ())), preferred_element_type=jnp.float32)
        scores = jnp.where(seen, scores * HEAD ** (-0.5), NEG_FILL)
        expanded = jnp.exp(scores - jnp.max(scores, axis=-1, keepdims=True))
        probs = (expanded / jnp.sum(expanded, axis=-1, keepdims=True)).astype(jnp.bfloat16)
        attended = jnp.dot(probs, v, preferred_element_type=jnp.float32)
        for h, cols in enumerate(heads):
            held = jnp.where(
                is_first, fresh_ref[fresh_rows, cols].astype(jnp.float32), incoming_ref[:, cols].astype(jnp.float32)
            )
            out_ref[:, cols] = (held + attended[h * tokens : (h + 1) * tokens]).astype(jnp.bfloat16)


def section(where, fresh, turn, incoming, gain, weights, seq_len, after=()):
    tokens, width = incoming.shape
    columns = 2 * weights[0].shape[1]
    return pl.pallas_call(
        functools.partial(section_kernel, seq_len, turn, len(after)),
        out_shape=jax.ShapeDtypeStruct((tokens, width), jnp.bfloat16),
        in_specs=[SCALARS] + [WHOLE] * 3 + [pl.BlockSpec(memory_space=pl.ANY)] * len(after) + [WHOLE] * len(weights),
        out_specs=WHOLE,
        scratch_shapes=[
            pltpu.VMEM((tokens, columns), jnp.bfloat16),
        ],
        compiler_params=pltpu.CompilerParams(vmem_limit_bytes=12 * MIB),
        cost_estimate=pl.CostEstimate(
            flops=2 * tokens * width * columns, bytes_accessed=width * columns * 2, transcendentals=0
        ),
        name="section",
    )(where, fresh, incoming, gain, *after, *weights)


def head_kernel(
    first_batch,
    length,
    sources,
    local_ref,
    pos_ref,
    valid_ref,
    at_ref,
    gain_ref,
    lang_ref,
    target_ref,
    teacher_ref,
    head_ref,
    *refs,
):
    source_refs = refs[:sources]
    out_ref = refs[-1]
    earlier = out_ref.shape[0] - 8
    out_ref[...] = jnp.zeros_like(out_ref)
    if earlier:
        out_ref[:earlier] = refs[sources][...]
    tokens, width = source_refs[0].shape
    batches = tokens // length
    slots = local_ref.shape[0] // (lang_ref.shape[0] // length)
    langs = slots // CAP
    picked = source_refs[0][...].astype(jnp.float32)
    for i in range(1, sources):
        picked = jnp.where(at_ref[0] == i, source_refs[i][...].astype(jnp.float32), picked)
    mean_sq = jnp.mean(picked * picked, axis=-1, keepdims=True)
    hidden = (picked * lax.rsqrt(mean_sq + EPSILON) * gain_ref[...]).astype(jnp.bfloat16)
    shape = (length, BLOCK)
    lane = lax.broadcasted_iota(jnp.int32, shape, 1)
    for b in range(batches):
        m = first_batch + b
        rows = slice(m * length, (m + 1) * length)
        lang = lang_ref[rows]
        target = target_ref[rows]
        block = jnp.concatenate(
            [
                head_ref[:, pl.ds(pl.multiple_of(local_ref[m * slots + i] * BLOCK, BLOCK), BLOCK)]
                for i in range(slots)
            ],
            axis=1,
        )
        every = jnp.dot(hidden[b * length : (b + 1) * length], block, preferred_element_type=jnp.float32)
        kept = []
        for c in range(CAP):
            logits = jnp.zeros(shape, jnp.float32)
            probs = jnp.zeros(shape, jnp.float32)
            valid = jnp.zeros(lang.shape, jnp.int32)
            pos = jnp.zeros(lang.shape, jnp.int32)
            for l in range(langs):
                at = l * CAP + c
                here = lang == l
                slot_pos = pos_ref[m * slots + at]
                cols = pl.ds(pl.multiple_of(slot_pos * BLOCK, BLOCK), BLOCK)
                logits = jnp.where(here, every[:, at * BLOCK : (at + 1) * BLOCK], logits)
                probs = jnp.where(here, teacher_ref[rows, cols].astype(jnp.float32), probs)
                valid = jnp.where(here, valid_ref[m * slots + at], valid)
                pos = jnp.where(here, slot_pos, pos)
            kept.append((logits, probs, valid == 1, pos))
        row_max = functools.reduce(
            jnp.maximum,
            [jnp.max(jnp.where(v, x, NEG_FILL), axis=-1, keepdims=True) for x, _, v, _ in kept],
        )
        total = jnp.zeros_like(row_max)
        cross = jnp.zeros_like(row_max)
        hit_sum = jnp.zeros_like(row_max)
        for x, p, v, pos in kept:
            total += jnp.sum(jnp.where(v, jnp.exp(jnp.where(v, x, NEG_FILL) - row_max), 0.0), axis=-1, keepdims=True)
            cross += jnp.sum(jnp.where(v, p * x, 0.0), axis=-1, keepdims=True)
            hit = v & (pos * BLOCK + lane == target)
            hit_sum += jnp.sum(jnp.where(hit, x, 0.0), axis=-1, keepdims=True)
        teach = teacher_ref[rows].astype(jnp.float32)
        self_sum = jnp.sum(teach * jnp.log(teach), axis=-1, keepdims=True)
        prob_sum = jnp.sum(teach, axis=-1, keepdims=True)
        packed = jnp.zeros(shape, jnp.float32)
        for i, value in enumerate((row_max, total, cross, hit_sum, self_sum, prob_sum)):
            packed = jnp.where(lane == i, value, packed)
        out_ref[earlier:, b * length : (b + 1) * length] = packed.T[:8]


def head_stats(first_batch, lanes, length, scalars, gain, langs_col, targets_col, teacher, head, sources, earlier):
    tokens, width = sources[0].shape
    slots = scalars[0].shape[0] * length // langs_col.shape[0]
    more = [] if earlier is None else [earlier]
    rows = 8 + (0 if earlier is None else earlier.shape[0])
    flops = 2 * tokens * width * slots * BLOCK
    return pl.pallas_call(
        functools.partial(head_kernel, first_batch, length, len(sources)),
        out_shape=jax.ShapeDtypeStruct((rows, lanes), jnp.float32),
        in_specs=[SCALARS] * 4 + [WHOLE] * (5 + len(sources) + len(more)),
        out_specs=WHOLE,
        compiler_params=pltpu.CompilerParams(vmem_limit_bytes=12 * MIB),
        cost_estimate=pl.CostEstimate(flops=flops, bytes_accessed=4 * MIB, transcendentals=0),
        name="head_stats",
    )(*scalars, gain, langs_col, targets_col, teacher, head, *sources, *more)


def join_kernel(length, sizes, *refs):
    stats_refs = refs[:-2]
    kl_ref, ce_ref = refs[-2:]
    row = 0
    for k, size in enumerate(sizes):
        stats = [ref[8 * k : 8 * k + 8, :] for ref in stats_refs]
        row_max = functools.reduce(jnp.maximum, [s[0:1] for s in stats])
        total = sum(s[1:2] * jnp.exp(s[0:1] - row_max) for s in stats)
        cross = sum(s[2:3] for s in stats)
        hit = sum(s[3:4] for s in stats)
        log_total = row_max + jnp.log(total)
        kl = stats[0][4:5] - cross + stats[0][5:6] * log_total
        ce = log_total - hit
        for b in range(size):
            kl_ref[row : row + 1] = kl[:, b * length : (b + 1) * length]
            ce_ref[row : row + 1] = ce[:, b * length : (b + 1) * length]
            row += 1


def joined(stats, length, sizes):
    out = jax.ShapeDtypeStruct((sum(sizes), length), jnp.float32)
    return pl.pallas_call(
        functools.partial(join_kernel, length, sizes),
        out_shape=(out, out),
        in_specs=[WHOLE] * len(stats),
        out_specs=(WHOLE, WHOLE),
        name="join",
    )(*stats)


def shifted(value, axis, step, first, last):
    return lax.ppermute(value, axis, [(s, s + step) for s in range(first, last)])


def on_device(
    layer_input,
    attn_gain,
    qkv_weight,
    final_gain,
    head_weight,
    vocab_blocks,
    languages,
    targets,
    teacher,
):
    seg = lax.axis_index("segment")
    count = lax.axis_size("segment")
    batches, _, length, width = layer_input.shape
    steps = len(CHUNKS) + HOP * (count - 1)
    unrolled = sum(CHUNKS) == batches and steps + count <= UNROLL_LIMIT
    sizes = CHUNKS if unrolled else (1,) * batches
    chunks = len(sizes)
    starts = [sum(sizes[:k]) for k in range(chunks)]
    where = jnp.stack(
        [(seg == 0).astype(jnp.int32), lax.axis_index("groups"), lax.axis_index("dp")]
    ).astype(jnp.int32)
    weights, crossed = gathered_weight(qkv_weight[0], where)
    head_in, _ = lax.optimization_barrier((head_weight, crossed))
    head = lax.all_gather(head_in, "dp", axis=0, tiled=True)
    fresh = layer_input.reshape(batches * length, width)

    list_len = vocab_blocks.shape[2]
    owned = vocab_blocks // VB_SEGMENT == seg
    order = jnp.cumsum(owned.astype(jnp.int32), axis=-1) - 1
    slot_ids = jnp.arange(CAP, dtype=jnp.int32)
    slot_hit = owned[:, :, None, :] & (order[:, :, None, :] == slot_ids[None, None, :, None])
    valid = jnp.any(slot_hit, axis=-1).astype(jnp.int32).reshape(-1)
    pos = jnp.sum(jnp.where(slot_hit, jnp.arange(list_len, dtype=jnp.int32), 0), axis=-1).reshape(-1)
    local = jnp.sum(jnp.where(slot_hit, vocab_blocks[:, :, None, :] % VB_SEGMENT, 0), axis=-1).reshape(-1)

    if unrolled:
        arrived = []
        previous = []
        sources = []
        moving = [[] for _ in range(steps + HOP)]
        for t in range(steps):
            k = min(t, chunks - 1)
            spare = jnp.zeros((sizes[k] * length, width), jnp.bfloat16)
            rows = section(
                where,
                fresh,
                starts[k] * length,
                arrived[t - HOP] if t >= HOP else spare,
                attn_gain,
                weights,
                length,
                previous + [h[-1] for h in moving[t]],
            )
            previous = [rows]
            arrived.append(shifted(rows, "segment", 1, 0, count - 1) if t + HOP < steps else None)
            going = moving[t]
            if t >= steps - chunks:
                sources.append([rows])
                going = [sources[-1]] + going
            for hops in going:
                if len(hops) < count and t < steps - 1:
                    src = count - len(hops)
                    hops.append(shifted(hops[-1], "segment", -1, src, src + 1))
                    moving[t + BACK].append(hops)
        last = sources[-1][0]
        for hops in sources[:-1]:
            while len(hops) < count:
                src = count - len(hops)
                passing, _ = lax.optimization_barrier((hops[-1], last))
                hops.append(shifted(passing, "segment", -1, src, src + 1))
        direct = [
            lax.ppermute(last, "segment", [(count - 1, count - 1 - j)]) for j in range(count - 1, 0, -1)
        ]
        sources[-1] = [last] + direct[::-1]
        at = (count - 1 - seg).astype(jnp.int32).reshape(1)
    else:

        def turn(t, state):
            incoming, kept = state
            here = jnp.concatenate([where, jnp.minimum(t, chunks - 1).astype(jnp.int32).reshape(1)])
            rows = section(here, fresh, None, incoming, attn_gain, weights, length)
            kept = lax.dynamic_update_index_in_dim(kept, rows, jnp.clip(t - (count - 1), 0, chunks - 1), 0)
            return shifted(rows, "segment", 1, 0, count - 1), kept

        zeros = jnp.zeros((length, width), jnp.bfloat16)
        _, kept = lax.fori_loop(
            0, chunks + count - 1, turn, (zeros, jnp.zeros((chunks, length, width), jnp.bfloat16))
        )

        def back(j, value):
            moved = shifted(value, "segment", -1, 1, count)
            return jnp.where(seg == count - 1 - j, moved, value)

        kept = lax.fori_loop(1, count, back, kept)
        sources = [[kept[k]] for k in range(chunks)]
        at = jnp.zeros((1,), jnp.int32)

    stats = None
    for k in range(chunks):
        stats = head_stats(
            starts[k],
            max(sizes) * length,
            length,
            (local, pos, valid, at),
            final_gain.reshape(1, width),
            languages.reshape(batches * length, 1),
            targets.reshape(batches * length, 1),
            teacher.reshape(batches * length, -1),
            head,
            sources[k],
            stats,
        )
    if unrolled:
        every = [stats] + [
            lax.ppermute(stats, "segment", [(s, (s + j) % count) for s in range(count)])
            for j in range(1, count)
        ]
    else:
        gathered = lax.all_gather(stats, "segment")
        every = [gathered[s] for s in range(count)]
    kl, ce = joined(every, length, sizes)
    return kl[:, None], ce[:, None]


def solution(mesh):
    return jax.shard_map(
        on_device,
        mesh=mesh,
        in_specs=(
            P("groups", "dp", None, None),
            P("segment", None),
            P("segment", "dp", None),
            P(),
            P("dp", "segment"),
            P("groups", None, None),
            P("groups", "dp", None),
            P("groups", "dp", None),
            P("groups", "dp", None, None),
        ),
        out_specs=(P("groups", "dp", None), P("groups", "dp", None)),
        check_vma=False,
    )
```
